32 devices in a mesh: pipe: 4 (over y, x), expert: 8 (over z, core).
Axes of the slice: x: 2, y: 2, z: 4, core: 2. Of those that a mesh axis runs over, the one named last changes fastest.
Arguments:
- out_grad: bfloat16 [4, 1, 1024, 1024], P('pipe', None, 'expert'), may hold values from -6 to 6
- gate_weights: float32 [4, 1, 1024, 8], P('pipe', None, 'expert'), may hold values from 0.05 to 1
- routes: int32 [4, 1, 1024, 8], P('pipe', None, 'expert'), may hold values from 0 to 7, as said below
- hidden_act: bfloat16 [4, 1, 8, 1024, 512], P('pipe', None, 'expert'), may hold values from -0.59765625 to 0.59765625
- down_weight: bfloat16 [4, 8, 256, 1024], P('pipe', 'expert'), may hold values from -0.1875 to 0.1875
- block_scales: float32 [4, 8, 2, 8], P('pipe', 'expert'), may hold values from 0.25 to 4
Outputs:
- hidden_grad: bfloat16 [4, 1, 8, 1024, 512], P('pipe', None, 'expert')
- weight_grad: bfloat16 [4, 8, 256, 1024], P('pipe', 'expert')
The draws below stay inside these ranges and needn't reach their ends.
Inputs may be any that keep to these rules, and one draw needn't show every extreme that they name: `routes`: each token names 8 different experts. Within one section and one micro-batch, the 128 tokens of each aligned block name every expert exactly 128 times.
All inputs are finite; a program needn't handle non-finite values.
Results may differ from the reference program's by a relative error of at most 0.0075.
Values may be sent and summed in bfloat16 or wider, within the bound.
A program may use at most 64 MiB of HBM per device.

```python
import math
import jax
import jax.numpy as jnp
from jax import lax

D = 1024
FF = 512
TOP = 8
QBLOCK = 128
MB = 1
TOK_MB = 128
EXPERTS = 8
TOKENS = 1024
CAP = 128
SLOTS = 1024
N_PIPE = 4
N_EXPERT = 8


def draw_routes(key, part):
    block_count = N_PIPE * MB * (TOKENS // TOK_MB)
    band_width = EXPERTS // TOP
    base_key = jax.random.fold_in(key, 11)
    column_key, label_key = jax.random.split(base_key)
    column_keys = jax.random.split(column_key, block_count * TOP)
    orders = jax.vmap(lambda single: jax.random.permutation(single, TOK_MB))(column_keys)
    orders = orders.reshape(block_count, TOP, TOK_MB).astype(jnp.int32)
    within_band = orders // CAP
    band_start = (jnp.arange(TOP, dtype=jnp.int32) * band_width)[None, :, None]
    labels = (within_band + band_start).reshape(block_count, TOP * TOK_MB)
    label_keys = jax.random.split(label_key, block_count)
    relabel = jax.vmap(lambda single: jax.random.permutation(single, EXPERTS))(label_keys).astype(jnp.int32)
    chosen = jnp.take_along_axis(relabel, labels, axis=1).reshape(block_count, TOP, TOK_MB)
    return chosen.transpose(0, 2, 1).reshape(N_PIPE, MB, TOKENS, TOP).astype(jnp.int32)


def block_scale(own_key, extent, cuts, low, largest):
    loudness, own = 1.0, jax.random.fold_in(own_key, 6)
    for axis_at, shards_of in cuts:
        heights = jnp.exp(jax.random.uniform(jax.random.fold_in(own, axis_at), (shards_of,), jnp.float32, low / len(cuts), largest / len(cuts)))
        loudness = loudness * jnp.repeat(heights, extent[axis_at] // shards_of).reshape([-1 if axis == axis_at else 1 for axis in range(len(extent))])
    return loudness


def gaussian(rng, dims, spread, most, cuts=(), kind=jnp.bfloat16):
    values = jax.random.normal(rng, dims, jnp.float32) * spread
    if len(cuts) > 0:
        values = block_scale(rng, dims, cuts, -0.22, 0.18) * values
    return jnp.clip(values, min=-most, max=most).astype(kind)


def setup_inputs(seed: int = 0) -> dict:
    seeds = jax.random.split(jax.random.key(seed), 7)
    return {
        "out_grad": gaussian(seeds[0], (N_PIPE, MB, TOKENS, D), 1.0, 6.0, ((0, 4), (2, 8))),
        "gate_weights": jnp.clip(0.05 + 0.95 * jax.random.uniform(seeds[1], (N_PIPE, MB, TOKENS, TOP), jnp.float32) ** block_scale(seeds[1], (N_PIPE, MB, TOKENS, TOP), ((0, 4), (2, 8)), -0.2, 0.2), 0.05, 1.0),
        "routes": draw_routes(jax.random.fold_in(seeds[6], 71), 0),
        "hidden_act": gaussian(seeds[3], (N_PIPE, MB, EXPERTS, SLOTS, FF), 0.1, 0.59765625, ((0, 4), (2, 8))),
        "down_weight": gaussian(seeds[4], (N_PIPE, EXPERTS, FF // 2, D), D ** -0.5, 0.1875, ((0, 4), (1, 8))),
        "block_scales": jnp.clip(jnp.exp(math.log(4.0) - 2.7725887 * jax.random.uniform(seeds[5], (N_PIPE, EXPERTS, FF // 2 // QBLOCK, D // QBLOCK), jnp.float32) ** block_scale(seeds[5], (N_PIPE, EXPERTS, FF // 2 // QBLOCK, D // QBLOCK), ((0, 4), (1, 8)), -0.2, 0.2)), 0.25, 4.0),
    }


def expand(scales):
    return jnp.repeat(jnp.repeat(scales, QBLOCK, axis=0), QBLOCK, axis=1)


def dispatch_rows(gradient, gate_rows, route_rows):
    scaled = (gate_rows[:, :, None] * gradient[:, None, :].astype(jnp.float32)).astype(jnp.bfloat16)
    scaled = scaled.reshape(TOKENS * TOP, D)
    expert_ids = route_rows.reshape(-1).astype(jnp.int32)
    onehot = (expert_ids[:, None] == jnp.arange(EXPERTS, dtype=jnp.int32)[None, :]).astype(jnp.int32)
    blocks = onehot.reshape(N_EXPERT, TOK_MB * TOP, EXPERTS)
    before = jnp.cumsum(blocks, axis=1) - blocks
    slot_rank = jnp.sum(before * blocks, axis=2).reshape(-1)
    source = jnp.arange(TOKENS * TOP, dtype=jnp.int32) // (TOK_MB * TOP)
    slot_index = (source * CAP + slot_rank).astype(jnp.int32)
    return jnp.zeros((EXPERTS, SLOTS, D), jnp.bfloat16).at[expert_ids, slot_index].set(scaled)


def reference(out_grad, gate_weights, routes, hidden_act, down_weight, block_scales):
    half_size = N_PIPE // 2
    half_rows = FF // 2

    def pair_block(pair_index):
        sections = jnp.stack([pair_index, pair_index + half_size]).astype(jnp.int32)
        dispatched = jax.vmap(jax.vmap(dispatch_rows))(out_grad[sections], gate_weights[sections], routes[sections])
        activations = hidden_act[sections]
        weights = down_weight[sections]
        scales = block_scales[sections]

        def expert_block(expert_index):
            slot_rows = dispatched[:, :, expert_index].astype(jnp.float32)
            dequant = (weights[:, expert_index].astype(jnp.float32) * jax.vmap(expand)(scales[:, expert_index])).astype(jnp.bfloat16)
            dequant = lax.optimization_barrier(dequant).astype(jnp.float32)
            whole = dequant.reshape(FF, D)
            hidden_grads = jnp.einsum("smrd,fd->smrf", slot_rows, whole).astype(jnp.bfloat16)
            section_sum = jnp.einsum("smrf,smrd->sfd", activations[:, :, expert_index].astype(jnp.float32), slot_rows)
            rounded = lax.optimization_barrier(section_sum.astype(jnp.bfloat16)).astype(jnp.float32)
            lower_half = (rounded[0, :half_rows] + rounded[1, :half_rows]).astype(jnp.bfloat16)
            upper_half = (rounded[0, half_rows:] + rounded[1, half_rows:]).astype(jnp.bfloat16)
            return hidden_grads, lower_half, upper_half

        return lax.map(expert_block, jnp.arange(EXPERTS, dtype=jnp.int32))

    hidden_grads, lower_half, upper_half = lax.map(pair_block, jnp.arange(half_size, dtype=jnp.int32))
    hidden_grad = hidden_grads.transpose(2, 0, 3, 1, 4, 5).reshape(N_PIPE, MB, EXPERTS, SLOTS, FF)
    weight_grad = jnp.concatenate([lower_half, upper_half], axis=0)
    return hidden_grad, weight_grad
```

```python
import functools

import jax
import jax.numpy as jnp
from jax import lax
from jax.experimental import pallas as pl
from jax.experimental.pallas import tpu as pltpu
from jax.sharding import PartitionSpec as P

QBLOCK = 128
WIDTH = 256
MESH = pl.DeviceIdType.MESH


def partner(block, axis):
    count = lax.axis_size(axis)
    route = [(place, (place + count // 2) % count) for place in range(count)]
    return lax.ppermute(block, axis, route)


def expand(scales):
    return jnp.repeat(jnp.repeat(scales, QBLOCK, axis=0), QBLOCK, axis=1)


def general(gradient, gate_rows, route_rows, activations, weight, scales):
    experts = lax.axis_size("expert")
    tok_count, features = gradient.shape
    top_count = route_rows.shape[1]
    capacity = tok_count * top_count // experts
    dequant_half = (weight.astype(jnp.float32) * expand(scales)).astype(jnp.bfloat16)
    named = route_rows[:, :, None] == jnp.arange(experts, dtype=jnp.int32)[None, None, :]
    gate_of = jnp.sum(jnp.where(named, gate_rows[:, :, None], 0.0), axis=1)
    member = jnp.any(named, axis=1)
    earlier = jnp.tril(jnp.ones((tok_count, tok_count), jnp.bfloat16), -1)
    rank = jnp.dot(earlier, member.astype(jnp.bfloat16), preferred_element_type=jnp.float32)
    rank = rank.astype(jnp.int32)
    places = jnp.arange(capacity, dtype=jnp.int32)[None, :, None]
    picked = member.T[:, None, :] & (rank.T[:, None, :] == places)
    slot_gate = jnp.sum(jnp.where(picked, gate_of.T[:, None, :], 0.0), axis=2)
    rows = jnp.dot(
        picked.reshape(experts * capacity, tok_count).astype(jnp.bfloat16),
        gradient,
        preferred_element_type=jnp.float32,
    )
    filled = (slot_gate.reshape(experts * capacity, 1) * rows).astype(jnp.bfloat16)
    received = lax.all_to_all(
        filled.reshape(experts, capacity, features),
        "expert",
        split_axis=0,
        concat_axis=0,
        tiled=True,
    ).reshape(experts * capacity, features)
    half_size = lax.axis_size("pipe") // 2
    upper_half = (lax.axis_index("pipe") >= half_size).astype(jnp.int32)
    half_rows = dequant_half.shape[0]
    other_half = partner(dequant_half, "pipe")
    whole = jnp.where(
        upper_half == 1,
        jnp.concatenate([other_half, dequant_half], axis=0),
        jnp.concatenate([dequant_half, other_half], axis=0),
    )
    hidden = lax.dot_general(
        received, whole, (((1,), (1,)), ((), ())), preferred_element_type=jnp.float32
    ).astype(jnp.bfloat16)
    section_sum = lax.dot_general(
        activations, received, (((0,), (0,)), ((), ())), preferred_element_type=jnp.float32
    )
    their_part = lax.dynamic_slice_in_dim(
        section_sum, (1 - upper_half) * half_rows, half_rows, 0
    ).astype(jnp.bfloat16)
    received_part = partner(their_part, "pipe")
    own_part = lax.dynamic_slice_in_dim(section_sum, upper_half * half_rows, half_rows, 0)
    rounded = lax.optimization_barrier(own_part.astype(jnp.bfloat16)).astype(jnp.float32)
    weight_grad = (rounded + received_part.astype(jnp.float32)).astype(jnp.bfloat16)
    return hidden, weight_grad


def kernel(
    sections, experts, gates_ref, routes_ref, scales_ref, x_hbm, act_hbm, weight_hbm,
    hidden_hbm, grad_hbm,
    x_own, act, act_t, weight, whole, got, scaled, gate_out, gate_in, gate_wide,
    theirs, ours, arrived, hidden, grad,
    load_sem, store_sem, row_send, row_recv, gate_send, gate_recv, w_send, w_recv, p_send, p_recv,
):
    section = lax.axis_index("pipe")
    me = lax.axis_index("expert")
    pair = lax.rem(section + sections // 2, sections)
    upper = section // (sections // 2)
    high, core = me // 2, lax.rem(me, 2)
    sibling = me + 1 - 2 * core
    last = experts // 2 - 1
    tokens, features = x_hbm.shape
    chunks = features // WIDTH
    slots, wide = act_hbm.shape
    half = wide // 2

    def rows_of(block):
        return pl.ds(pl.multiple_of(block * tokens, tokens), tokens)

    def columns(chunk):
        return pl.ds(pl.multiple_of(chunk * WIDTH, WIDTH), WIDTH)

    load_x = pltpu.make_async_copy(x_hbm, x_own, load_sem.at[0])
    load_w = pltpu.make_async_copy(weight_hbm, weight, load_sem.at[1])
    load_a = pltpu.make_async_copy(act_hbm, act, load_sem.at[2])
    load_x.start()
    load_w.start()
    load_a.start()

    barrier = pltpu.get_barrier_semaphore()
    for step in range(1, experts):
        peer = lax.rem(me + step, experts)
        pl.semaphore_signal(barrier, inc=1, device_id=(section, peer), device_id_type=MESH)
    pl.semaphore_signal(barrier, inc=1, device_id=(pair, me), device_id_type=MESH)

    for expert in range(experts):
        gate_out[expert] = jnp.sum(
            jnp.where(routes_ref[...] == expert, gates_ref[...], 0.0), axis=0, keepdims=True
        )
    gate_in[me] = gate_out[me]
    load_x.wait()
    pl.semaphore_wait(barrier, experts)

    def move(block, chunk, way, peer, from_own=False):
        source = x_own.at[:, columns(chunk)] if from_own else got.at[chunk, rows_of(block)]
        return pltpu.make_async_remote_copy(
            src_ref=source,
            dst_ref=got.at[chunk, rows_of(block)],
            send_sem=row_send.at[way, block, chunk],
            recv_sem=row_recv.at[block, chunk],
            device_id=(section, peer),
            device_id_type=MESH,
        )

    def send_own(chunk):
        @pl.when(high > 0)
        def _():
            move(me, chunk, 0, me - 2, True).start()

        @pl.when(high < last)
        def _():
            move(me, chunk, 1, me + 2, True).start()

        move(me, chunk, 2, sibling, True).start()

    def gate_copy(peer, source):
        return pltpu.make_async_remote_copy(
            src_ref=gate_out.at[peer],
            dst_ref=gate_in.at[source],
            send_sem=gate_send.at[peer],
            recv_sem=gate_recv.at[source],
            device_id=(section, peer),
            device_id_type=MESH,
        )

    def weight_copy(chunk, which):
        rows = pl.ds(pl.multiple_of(which * half, half), half)
        return pltpu.make_async_remote_copy(
            src_ref=whole.at[chunk, rows],
            dst_ref=whole.at[chunk, rows],
            send_sem=w_send.at[chunk],
            recv_sem=w_recv.at[chunk],
            device_id=(pair, me),
            device_id_type=MESH,
        )

    def part_copy(chunk):
        return pltpu.make_async_remote_copy(
            src_ref=theirs.at[chunk],
            dst_ref=arrived.at[chunk],
            send_sem=p_send.at[chunk],
            recv_sem=p_recv.at[chunk],
            device_id=(pair, me),
            device_id_type=MESH,
        )

    for step in range(1, experts):
        gate_copy(lax.rem(me + step, experts), me).start()
    send_own(0)
    send_own(1)

    load_w.wait()
    for chunk in range(chunks):
        for row in range(half // QBLOCK):
            for part in range(WIDTH // QBLOCK):
                column = chunk * (WIDTH // QBLOCK) + part
                piece = weight[
                    row * QBLOCK : (row + 1) * QBLOCK, column * QBLOCK : (column + 1) * QBLOCK
                ]
                whole[
                    chunk,
                    pl.ds(pl.multiple_of(upper * half + row * QBLOCK, QBLOCK), QBLOCK),
                    part * QBLOCK : (part + 1) * QBLOCK,
                ] = (piece.astype(jnp.float32) * scales_ref[row, column]).astype(jnp.bfloat16)
        weight_copy(chunk, upper).start()

    load_a.wait()

    @pl.loop(0, slots // WIDTH)
    def _(tile):
        at = pl.ds(pl.multiple_of(tile * WIDTH, WIDTH), WIDTH)
        act_t[:, at] = act[at, :].T

    for step in range(1, experts):
        source = lax.rem(me + step, experts)
        gate_copy(source, source).wait_recv()

    for block in range(experts):
        gate_wide[block] = jnp.broadcast_to(gate_in[block], (QBLOCK, tokens)).T

    def apply_gate(block, chunk, rows):
        for part in range(WIDTH // QBLOCK):
            at = slice(part * QBLOCK, (part + 1) * QBLOCK)
            scaled[chunk, rows_of(block), at] = (
                gate_wide[block] * rows[:, at].astype(jnp.float32)
            ).astype(jnp.bfloat16)

    def landed(block, chunk):
        move(block, chunk, 2, sibling).wait_recv()

    def gate_landed(block, chunk):
        apply_gate(block, chunk, got[chunk, rows_of(block)])

    @pl.loop(0, chunks)
    def _(chunk):
        apply_gate(me, chunk, x_own[:, columns(chunk)])
        for step in range(1, experts // 2):
            @pl.when(high >= step)
            def _():
                block = me - 2 * step
                landed(block, chunk)

                @pl.when(high < last)
                def _():
                    move(block, chunk, 1, me + 2).start()

                move(block, chunk, 2, sibling).start()

            @pl.when(high + step <= last)
            def _():
                block = me + 2 * step
                landed(block, chunk)

                @pl.when(high > 0)
                def _():
                    move(block, chunk, 0, me - 2).start()

                move(block, chunk, 2, sibling).start()

            if step == 1:
                landed(sibling, chunk)
                gate_landed(sibling, chunk)

            @pl.when(high >= step)
            def _():
                block = me - 2 * step
                gate_landed(block, chunk)

            @pl.when(high + step <= last)
            def _():
                block = me + 2 * step
                gate_landed(block, chunk)

        @pl.when(chunk + 2 < chunks)
        def _():
            send_own(chunk + 2)

        for step in range(1, experts // 2):
            @pl.when(high >= step)
            def _():
                block = sibling - 2 * step
                landed(block, chunk)
                gate_landed(block, chunk)

            @pl.when(high + step <= last)
            def _():
                block = sibling + 2 * step
                landed(block, chunk)
                gate_landed(block, chunk)

        their_rows = pl.ds(pl.multiple_of((1 - upper) * half, half), half)
        theirs[chunk] = jnp.dot(
            act_t[their_rows, :], scaled[chunk], preferred_element_type=jnp.float32
        ).astype(jnp.bfloat16)
        part_copy(chunk).start()
        our_rows = pl.ds(pl.multiple_of(upper * half, half), half)
        ours[chunk] = jnp.dot(
            act_t[our_rows, :], scaled[chunk], preferred_element_type=jnp.float32
        ).astype(jnp.bfloat16)

    for chunk in range(chunks):
        weight_copy(chunk, 1 - upper).wait_recv()

    @pl.loop(0, slots // WIDTH)
    def _(tile):
        at = pl.ds(pl.multiple_of(tile * WIDTH, WIDTH), WIDTH)
        total = None
        for chunk in range(chunks):
            term = lax.dot_general(
                scaled[chunk, at],
                whole[chunk],
                (((1,), (1,)), ((), ())),
                preferred_element_type=jnp.float32,
            )
            total = term if total is None else total + term
        hidden[at, :] = total.astype(jnp.bfloat16)

    store_h = pltpu.make_async_copy(hidden, hidden_hbm, store_sem.at[0])
    store_h.start()

    for chunk in range(chunks):
        part_copy(chunk).wait_recv()
        grad[:, chunk * WIDTH : (chunk + 1) * WIDTH] = (
            ours[chunk].astype(jnp.float32) + arrived[chunk].astype(jnp.float32)
        ).astype(jnp.bfloat16)
    store_g = pltpu.make_async_copy(grad, grad_hbm, store_sem.at[1])
    store_g.start()

    for step in range(1, experts):
        gate_copy(lax.rem(me + step, experts), me).wait_send()

    @pl.loop(0, chunks)
    def _(chunk):
        part_copy(chunk).wait_send()
        weight_copy(chunk, upper).wait_send()

        @pl.when(high > 0)
        def _():
            move(me, chunk, 0, me - 2, True).wait_send()

        @pl.when(high < last)
        def _():
            move(me, chunk, 1, me + 2, True).wait_send()

        move(me, chunk, 2, sibling, True).wait_send()
        for step in range(1, experts // 2):
            @pl.when(high >= step)
            def _():
                block = me - 2 * step

                @pl.when(high < last)
                def _():
                    move(block, chunk, 1, me + 2).wait_send()

                move(block, chunk, 2, sibling).wait_send()

            @pl.when(high + step <= last)
            def _():
                block = me + 2 * step

                @pl.when(high > 0)
                def _():
                    move(block, chunk, 0, me - 2).wait_send()

                move(block, chunk, 2, sibling).wait_send()

    store_h.wait()
    store_g.wait()


def every_expert(gradient, gate_rows, route_rows, activations, weight, scales):
    sections, experts = lax.axis_size("pipe"), lax.axis_size("expert")
    tokens, features = gradient.shape
    slots, wide = activations.shape
    half = weight.shape[0]
    chunks = features // WIDTH
    bf16, f32 = jnp.bfloat16, jnp.float32
    dma = pltpu.SemaphoreType.DMA
    anywhere = pl.BlockSpec(memory_space=pl.ANY)
    vmem = pl.BlockSpec(memory_space=pltpu.VMEM)
    return pl.pallas_call(
        functools.partial(kernel, sections, experts),
        out_shape=(
            jax.ShapeDtypeStruct((slots, wide), bf16),
            jax.ShapeDtypeStruct((half, features), bf16),
        ),
        in_specs=[
            vmem, vmem, pl.BlockSpec(memory_space=pltpu.SMEM), anywhere, anywhere, anywhere,
        ],
        out_specs=(anywhere, anywhere),
        scratch_shapes=[
            pltpu.VMEM((tokens, features), bf16),
            pltpu.VMEM((slots, wide), bf16),
            pltpu.VMEM((wide, slots), bf16),
            pltpu.VMEM((half, features), bf16),
            pltpu.VMEM((chunks, wide, WIDTH), bf16),
            pltpu.VMEM((chunks, slots, WIDTH), bf16),
            pltpu.VMEM((chunks, slots, WIDTH), bf16),
            pltpu.VMEM((experts, 1, tokens), f32),
            pltpu.VMEM((experts, 1, tokens), f32),
            pltpu.VMEM((experts, tokens, QBLOCK), f32),
            pltpu.VMEM((chunks, half, WIDTH), bf16),
            pltpu.VMEM((chunks, half, WIDTH), bf16),
            pltpu.VMEM((chunks, half, WIDTH), bf16),
            pltpu.VMEM((slots, wide), bf16),
            pltpu.VMEM((half, features), bf16),
            dma((3,)),
            dma((2,)),
            dma((3, experts, chunks)),
            dma((experts, chunks)),
            dma((experts,)),
            dma((experts,)),
            dma((chunks,)),
            dma((chunks,)),
            dma((chunks,)),
            dma((chunks,)),
        ],
        compiler_params=pltpu.CompilerParams(
            collective_id=0, has_side_effects=True, vmem_limit_bytes=48 * 2**20
        ),
        cost_estimate=pl.CostEstimate(
            flops=4 * slots * wide * features,
            bytes_accessed=4 * slots * wide + 6 * half * features,
            transcendentals=0,
        ),
    )(gate_rows.T, route_rows.T, scales, gradient, activations, weight)


def on_device(out_grad, gate_weights, routes, hidden_act, down_weight, block_scales):
    experts, sections = lax.axis_size("expert"), lax.axis_size("pipe")
    gradient, gate_rows, route_rows = out_grad[0, 0], gate_weights[0, 0], routes[0, 0]
    weight, scales = down_weight[0, 0], block_scales[0, 0]
    tokens, features = gradient.shape
    dense = (
        experts == route_rows.shape[1]
        and experts >= 4
        and experts % 2 == 0
        and sections % 2 == 0
        and tokens == QBLOCK
        and features % WIDTH == 0
        and features // WIDTH >= 2
        and weight.shape[0] % QBLOCK == 0
    )
    form = every_expert if dense else general
    hidden, weight_grad = form(
        gradient, gate_rows, route_rows, hidden_act[0, 0, 0], weight, scales
    )
    return hidden[None, None, None], weight_grad[None, None]


def solution(mesh):
    in_specs = (
        P("pipe", None, "expert", None),
        P("pipe", None, "expert", None),
        P("pipe", None, "expert", None),
        P("pipe", None, "expert", None, None),
        P("pipe", "expert", None, None),
        P("pipe", "expert", None, None),
    )
    out_specs = (P("pipe", None, "expert", None, None), P("pipe", "expert", None, None))
    return jax.shard_map(
        on_device, mesh=mesh, in_specs=in_specs, out_specs=out_specs, check_vma=False
    )
```

```python
import functools

import jax
import jax.numpy as jnp
from jax import lax
from jax.experimental import pallas as pl
from jax.experimental.pallas import tpu as pltpu
from jax.sharding import PartitionSpec as P

QBLOCK = 128
WIDTH = 256
ROOM = 63 * 2**20
MESH = pl.DeviceIdType.MESH


def partner(block, axis):
    count = lax.axis_size(axis)
    route = [(place, (place + count // 2) % count) for place in range(count)]
    return lax.ppermute(block, axis, route)


def expand(scales):
    return jnp.repeat(jnp.repeat(scales, QBLOCK, axis=0), QBLOCK, axis=1)


def general(gradient, gate_rows, route_rows, activations, weight, scales):
    experts = lax.axis_size("expert")
    tok_count, features = gradient.shape
    top_count = route_rows.shape[1]
    capacity = tok_count * top_count // experts
    dequant_half = (weight.astype(jnp.float32) * expand(scales)).astype(jnp.bfloat16)
    named = route_rows[:, :, None] == jnp.arange(experts, dtype=jnp.int32)[None, None, :]
    gate_of = jnp.sum(jnp.where(named, gate_rows[:, :, None], 0.0), axis=1)
    member = jnp.any(named, axis=1)
    earlier = jnp.tril(jnp.ones((tok_count, tok_count), jnp.bfloat16), -1)
    rank = jnp.dot(earlier, member.astype(jnp.bfloat16), preferred_element_type=jnp.float32)
    rank = rank.astype(jnp.int32)
    places = jnp.arange(capacity, dtype=jnp.int32)[None, :, None]
    picked = member.T[:, None, :] & (rank.T[:, None, :] == places)
    slot_gate = jnp.sum(jnp.where(picked, gate_of.T[:, None, :], 0.0), axis=2)
    rows = jnp.dot(
        picked.reshape(experts * capacity, tok_count).astype(jnp.bfloat16),
        gradient,
        preferred_element_type=jnp.float32,
    )
    filled = (slot_gate.reshape(experts * capacity, 1) * rows).astype(jnp.bfloat16)
    received = lax.all_to_all(
        filled.reshape(experts, capacity, features),
        "expert",
        split_axis=0,
        concat_axis=0,
        tiled=True,
    ).reshape(experts * capacity, features)
    half_size = lax.axis_size("pipe") // 2
    upper_half = (lax.axis_index("pipe") >= half_size).astype(jnp.int32)
    half_rows = dequant_half.shape[0]
    other_half = partner(dequant_half, "pipe")
    whole = jnp.where(
        upper_half == 1,
        jnp.concatenate([other_half, dequant_half], axis=0),
        jnp.concatenate([dequant_half, other_half], axis=0),
    )
    hidden = lax.dot_general(
        received, whole, (((1,), (1,)), ((), ())), preferred_element_type=jnp.float32
    ).astype(jnp.bfloat16)
    section_sum = lax.dot_general(
        activations, received, (((0,), (0,)), ((), ())), preferred_element_type=jnp.float32
    )
    their_part = lax.dynamic_slice_in_dim(
        section_sum, (1 - upper_half) * half_rows, half_rows, 0
    ).astype(jnp.bfloat16)
    received_part = partner(their_part, "pipe")
    own_part = lax.dynamic_slice_in_dim(section_sum, upper_half * half_rows, half_rows, 0)
    rounded = lax.optimization_barrier(own_part.astype(jnp.bfloat16)).astype(jnp.float32)
    weight_grad = (rounded + received_part.astype(jnp.float32)).astype(jnp.bfloat16)
    return hidden, weight_grad


def kernel(
    sections, experts, gates_hbm, routes_hbm, scales_hbm, x_hbm, act_hbm, weight_hbm,
    hidden_hbm, grad_hbm,
    gates_ref, routes_ref, scales_ref, hidden_ref, grad_ref, x_own, act, act_t, weight, whole, got, scaled, gate_out, gate_in, gate_wide,
    theirs, ours, arrived,
    load_sem, store_sem, row_send, row_recv, gate_send, gate_recv, w_send, w_recv, p_send, p_recv,
):
    section = lax.axis_index("pipe")
    me = lax.axis_index("expert")
    pair = lax.rem(section + sections // 2, sections)
    upper = section // (sections // 2)
    high, core = me // 2, lax.rem(me, 2)
    sibling = me + 1 - 2 * core
    last = experts // 2 - 1
    tokens, features = x_hbm.shape
    chunks = features // WIDTH
    slots, wide = act_hbm.shape
    half = wide // 2

    def rows_of(block):
        return pl.ds(pl.multiple_of(block * tokens, tokens), tokens)

    def columns(chunk):
        return pl.ds(pl.multiple_of(chunk * WIDTH, WIDTH), WIDTH)

    load_x = pltpu.make_async_copy(x_hbm, x_own, load_sem.at[0])
    load_w = pltpu.make_async_copy(weight_hbm, weight, load_sem.at[1])
    load_a = pltpu.make_async_copy(act_hbm, act, load_sem.at[2])
    load_g = pltpu.make_async_copy(gates_hbm, gates_ref, load_sem.at[3])
    load_r = pltpu.make_async_copy(routes_hbm, routes_ref, load_sem.at[4])
    load_s = pltpu.make_async_copy(scales_hbm, scales_ref, load_sem.at[5])
    for load in (load_x, load_w, load_s, load_g, load_r, load_a):
        load.start()

    barrier = pltpu.get_barrier_semaphore()
    for step in range(1, experts):
        peer = lax.rem(me + step, experts)
        pl.semaphore_signal(barrier, inc=1, device_id=(section, peer), device_id_type=MESH)
    pl.semaphore_signal(barrier, inc=1, device_id=(pair, me), device_id_type=MESH)

    load_x.wait()
    pl.semaphore_wait(barrier, experts)

    def move(block, chunk, way, peer, from_own=False):
        source = x_own.at[:, columns(chunk)] if from_own else got.at[chunk, rows_of(block)]
        return pltpu.make_async_remote_copy(
            src_ref=source,
            dst_ref=got.at[chunk, rows_of(block)],
            send_sem=row_send.at[way, block, chunk],
            recv_sem=row_recv.at[block, chunk],
            device_id=(section, peer),
            device_id_type=MESH,
        )

    def send_own(chunk):
        @pl.when(high > 0)
        def _():
            move(me, chunk, 0, me - 2, True).start()

        @pl.when(high < last)
        def _():
            move(me, chunk, 1, me + 2, True).start()

        move(me, chunk, 2, sibling, True).start()

    def gate_copy(peer, source):
        return pltpu.make_async_remote_copy(
            src_ref=gate_out.at[peer],
            dst_ref=gate_in.at[source],
            send_sem=gate_send.at[peer],
            recv_sem=gate_recv.at[source],
            device_id=(section, peer),
            device_id_type=MESH,
        )

    def weight_copy(chunk, which):
        rows = pl.ds(pl.multiple_of(which * half, half), half)
        return pltpu.make_async_remote_copy(
            src_ref=whole.at[chunk, rows],
            dst_ref=whole.at[chunk, rows],
            send_sem=w_send.at[chunk],
            recv_sem=w_recv.at[chunk],
            device_id=(pair, me),
            device_id_type=MESH,
        )

    def part_copy(chunk):
        return pltpu.make_async_remote_copy(
            src_ref=theirs.at[chunk],
            dst_ref=arrived.at[chunk],
            send_sem=p_send.at[chunk],
            recv_sem=p_recv.at[chunk],
            device_id=(pair, me),
            device_id_type=MESH,
        )

    send_own(0)
    send_own(1)

    load_w.wait()
    load_s.wait()
    for chunk in range(chunks):
        for row in range(half // QBLOCK):
            for part in range(WIDTH // QBLOCK):
                column = chunk * (WIDTH // QBLOCK) + part
                piece = weight[
                    row * QBLOCK : (row + 1) * QBLOCK, column * QBLOCK : (column + 1) * QBLOCK
                ]
                whole[
                    chunk,
                    pl.ds(pl.multiple_of(upper * half + row * QBLOCK, QBLOCK), QBLOCK),
                    part * QBLOCK : (part + 1) * QBLOCK,
                ] = (piece.astype(jnp.float32) * scales_ref[row, column]).astype(jnp.bfloat16)
        weight_copy(chunk, upper).start()

    load_g.wait()
    load_r.wait()
    for expert in range(experts):
        gate_out[expert] = jnp.sum(
            jnp.where(routes_ref[...] == expert, gates_ref[...], 0.0), axis=0, keepdims=True
        )
    gate_in[me] = gate_out[me]
    for step in range(1, experts):
        gate_copy(lax.rem(me + step, experts), me).start()

    load_a.wait()

    @pl.loop(0, slots // WIDTH)
    def _(tile):
        at = pl.ds(pl.multiple_of(tile * WIDTH, WIDTH), WIDTH)
        act_t[:, at] = act[at, :].T

    for step in range(1, experts):
        source = lax.rem(me + step, experts)
        gate_copy(source, source).wait_recv()

    for block in range(experts):
        gate_wide[block] = jnp.broadcast_to(gate_in[block], (QBLOCK, tokens)).T

    def apply_gate(block, chunk, rows):
        for part in range(WIDTH // QBLOCK):
            at = slice(part * QBLOCK, (part + 1) * QBLOCK)
            scaled[chunk, rows_of(block), at] = (
                gate_wide[block] * rows[:, at].astype(jnp.float32)
            ).astype(jnp.bfloat16)

    def landed(block, chunk):
        move(block, chunk, 2, sibling).wait_recv()

    def gate_landed(block, chunk):
        apply_gate(block, chunk, got[chunk, rows_of(block)])

    @pl.loop(0, chunks)
    def _(chunk):
        apply_gate(me, chunk, x_own[:, columns(chunk)])
        for step in range(1, experts // 2):
            @pl.when(high >= step)
            def _():
                block = me - 2 * step
                landed(block, chunk)

                @pl.when(high < last)
                def _():
                    move(block, chunk, 1, me + 2).start()

                move(block, chunk, 2, sibling).start()

            @pl.when(high + step <= last)
            def _():
                block = me + 2 * step
                landed(block, chunk)

                @pl.when(high > 0)
                def _():
                    move(block, chunk, 0, me - 2).start()

                move(block, chunk, 2, sibling).start()

            if step == 1:
                landed(sibling, chunk)
                gate_landed(sibling, chunk)

            @pl.when(high >= step)
            def _():
                block = me - 2 * step
                gate_landed(block, chunk)

            @pl.when(high + step <= last)
            def _():
                block = me + 2 * step
                gate_landed(block, chunk)

        @pl.when(chunk + 2 < chunks)
        def _():
            send_own(chunk + 2)

        for step in range(1, experts // 2):
            @pl.when(high >= step)
            def _():
                block = sibling - 2 * step
                landed(block, chunk)
                gate_landed(block, chunk)

            @pl.when(high + step <= last)
            def _():
                block = sibling + 2 * step
                landed(block, chunk)
                gate_landed(block, chunk)

        their_rows = pl.ds(pl.multiple_of((1 - upper) * half, half), half)
        theirs[chunk] = jnp.dot(
            act_t[their_rows, :], scaled[chunk], preferred_element_type=jnp.float32
        ).astype(jnp.bfloat16)
        part_copy(chunk).start()
        our_rows = pl.ds(pl.multiple_of(upper * half, half), half)
        ours[chunk] = jnp.dot(
            act_t[our_rows, :], scaled[chunk], preferred_element_type=jnp.float32
        ).astype(jnp.bfloat16)

    for chunk in range(chunks):
        weight_copy(chunk, 1 - upper).wait_recv()

    @pl.loop(0, slots // WIDTH)
    def _(tile):
        at = pl.ds(pl.multiple_of(tile * WIDTH, WIDTH), WIDTH)
        total = None
        for chunk in range(chunks):
            term = lax.dot_general(
                scaled[chunk, at],
                whole[chunk],
                (((1,), (1,)), ((), ())),
                preferred_element_type=jnp.float32,
            )
            total = term if total is None else total + term
        hidden_ref[at, :] = total.astype(jnp.bfloat16)

    store_h = pltpu.make_async_copy(hidden_ref, hidden_hbm, store_sem.at[0])
    store_h.start()

    for chunk in range(chunks):
        part_copy(chunk).wait_recv()
        grad_ref[:, chunk * WIDTH : (chunk + 1) * WIDTH] = (
            ours[chunk].astype(jnp.float32) + arrived[chunk].astype(jnp.float32)
        ).astype(jnp.bfloat16)
    store_g = pltpu.make_async_copy(grad_ref, grad_hbm, store_sem.at[1])
    store_g.start()

    for step in range(1, experts):
        gate_copy(lax.rem(me + step, experts), me).wait_send()

    @pl.loop(0, chunks)
    def _(chunk):
        part_copy(chunk).wait_send()
        weight_copy(chunk, upper).wait_send()

        @pl.when(high > 0)
        def _():
            move(me, chunk, 0, me - 2, True).wait_send()

        @pl.when(high < last)
        def _():
            move(me, chunk, 1, me + 2, True).wait_send()

        move(me, chunk, 2, sibling, True).wait_send()
        for step in range(1, experts // 2):
            @pl.when(high >= step)
            def _():
                block = me - 2 * step

                @pl.when(high < last)
                def _():
                    move(block, chunk, 1, me + 2).wait_send()

                move(block, chunk, 2, sibling).wait_send()

            @pl.when(high + step <= last)
            def _():
                block = me + 2 * step

                @pl.when(high > 0)
                def _():
                    move(block, chunk, 0, me - 2).wait_send()

                move(block, chunk, 2, sibling).wait_send()

    store_h.wait()
    store_g.wait()


def store(hidden_ref, grad_ref, hidden_hbm, grad_hbm, sem):
    copies = [
        pltpu.make_async_copy(hidden_ref, hidden_hbm, sem.at[0]),
        pltpu.make_async_copy(grad_ref, grad_hbm, sem.at[1]),
    ]
    for copy in copies:
        copy.start()
    for copy in copies:
        copy.wait()


def every_expert(gradient, gate_rows, route_rows, activations, weight, scales):
    sections, experts = lax.axis_size("pipe"), lax.axis_size("expert")
    tokens, features = gradient.shape
    slots, wide = activations.shape
    half = weight.shape[0]
    chunks = features // WIDTH
    bf16, f32 = jnp.bfloat16, jnp.float32
    dma = pltpu.SemaphoreType.DMA
    shapes = (
        jax.ShapeDtypeStruct((slots, wide), bf16),
        jax.ShapeDtypeStruct((half, features), bf16),
    )
    results = pl.pallas_call(
        functools.partial(kernel, sections, experts),
        out_shape=shapes,
        in_specs=[pl.BlockSpec(memory_space=pltpu.HBM)] * 6,
        out_specs=(pl.BlockSpec(memory_space=pltpu.HBM),) * 2,
        scratch_shapes=[
            pltpu.VMEM(gate_rows.shape[::-1], f32),
            pltpu.VMEM(route_rows.shape[::-1], jnp.int32),
            pltpu.SMEM(scales.shape, f32),
            pltpu.VMEM((slots, wide), bf16),
            pltpu.VMEM((half, features), bf16),
            pltpu.VMEM((tokens, features), bf16),
            pltpu.VMEM((slots, wide), bf16),
            pltpu.VMEM((wide, slots), bf16),
            pltpu.VMEM((half, features), bf16),
            pltpu.VMEM((chunks, wide, WIDTH), bf16),
            pltpu.VMEM((chunks, slots, WIDTH), bf16),
            pltpu.VMEM((chunks, slots, WIDTH), bf16),
            pltpu.VMEM((experts, 1, tokens), f32),
            pltpu.VMEM((experts, 1, tokens), f32),
            pltpu.VMEM((experts, tokens, QBLOCK), f32),
            pltpu.VMEM((chunks, half, WIDTH), bf16),
            pltpu.VMEM((chunks, half, WIDTH), bf16),
            pltpu.VMEM((chunks, half, WIDTH), bf16),
            dma((6,)),
            dma((2,)),
            dma((3, experts, chunks)),
            dma((experts, chunks)),
            dma((experts,)),
            dma((experts,)),
            dma((chunks,)),
            dma((chunks,)),
            dma((chunks,)),
            dma((chunks,)),
        ],
        compiler_params=pltpu.CompilerParams(
            collective_id=0, has_side_effects=True, vmem_limit_bytes=ROOM
        ),
        cost_estimate=pl.CostEstimate(
            flops=4 * slots * wide * features,
            bytes_accessed=4 * slots * wide + 6 * half * features,
            transcendentals=0,
        ),
    )(gate_rows.T, route_rows.T, scales, gradient, activations, weight)
    return pl.pallas_call(
        store,
        out_shape=shapes,
        in_specs=[pl.BlockSpec(memory_space=pltpu.HBM)] * 2,
        out_specs=(pl.BlockSpec(memory_space=pltpu.HBM),) * 2,
        scratch_shapes=[dma((2,))],
        compiler_params=pltpu.CompilerParams(vmem_limit_bytes=ROOM),
    )(*results)


def on_device(out_grad, gate_weights, routes, hidden_act, down_weight, block_scales):
    experts, sections = lax.axis_size("expert"), lax.axis_size("pipe")
    gradient, gate_rows, route_rows = out_grad[0, 0], gate_weights[0, 0], routes[0, 0]
    weight, scales = down_weight[0, 0], block_scales[0, 0]
    tokens, features = gradient.shape
    dense = (
        experts == route_rows.shape[1]
        and experts >= 4
        and experts % 2 == 0
        and sections % 2 == 0
        and tokens == QBLOCK
        and features % WIDTH == 0
        and features // WIDTH >= 2
        and weight.shape[0] % QBLOCK == 0
    )
    form = every_expert if dense else general
    hidden, weight_grad = form(
        gradient, gate_rows, route_rows, hidden_act[0, 0, 0], weight, scales
    )
    return hidden[None, None, None], weight_grad[None, None]


def solution(mesh):
    in_specs = (
        P("pipe", None, "expert", None),
        P("pipe", None, "expert", None),
        P("pipe", None, "expert", None),
        P("pipe", None, "expert", None, None),
        P("pipe", "expert", None, None),
        P("pipe", "expert", None, None),
    )
    out_specs = (P("pipe", None, "expert", None, None), P("pipe", "expert", None, None))
    return jax.shard_map(
        on_device, mesh=mesh, in_specs=in_specs, out_specs=out_specs, check_vma=False
    )
```

```python
import functools

import jax
import jax.numpy as jnp
from jax import lax
from jax.experimental import pallas as pl
from jax.experimental.pallas import tpu as pltpu
from jax.sharding import PartitionSpec as P

QBLOCK = 128
WIDTH = 256
PIECES = 4
ROOM = 63 * 2**20
MESH = pl.DeviceIdType.MESH


def partner(block, axis):
    count = lax.axis_size(axis)
    route = [(place, (place + count // 2) % count) for place in range(count)]
    return lax.ppermute(block, axis, route)


def expand(scales):
    return jnp.repeat(jnp.repeat(scales, QBLOCK, axis=0), QBLOCK, axis=1)


def general(gradient, gate_rows, route_rows, activations, weight, scales):
    experts = lax.axis_size("expert")
    tok_count, features = gradient.shape
    top_count = route_rows.shape[1]
    capacity = tok_count * top_count // experts
    dequant_half = (weight.astype(jnp.float32) * expand(scales)).astype(jnp.bfloat16)
    named = route_rows[:, :, None] == jnp.arange(experts, dtype=jnp.int32)[None, None, :]
    gate_of = jnp.sum(jnp.where(named, gate_rows[:, :, None], 0.0), axis=1)
    member = jnp.any(named, axis=1)
    earlier = jnp.tril(jnp.ones((tok_count, tok_count), jnp.bfloat16), -1)
    rank = jnp.dot(earlier, member.astype(jnp.bfloat16), preferred_element_type=jnp.float32)
    rank = rank.astype(jnp.int32)
    places = jnp.arange(capacity, dtype=jnp.int32)[None, :, None]
    picked = member.T[:, None, :] & (rank.T[:, None, :] == places)
    slot_gate = jnp.sum(jnp.where(picked, gate_of.T[:, None, :], 0.0), axis=2)
    rows = jnp.dot(
        picked.reshape(experts * capacity, tok_count).astype(jnp.bfloat16),
        gradient,
        preferred_element_type=jnp.float32,
    )
    filled = (slot_gate.reshape(experts * capacity, 1) * rows).astype(jnp.bfloat16)
    received = lax.all_to_all(
        filled.reshape(experts, capacity, features),
        "expert",
        split_axis=0,
        concat_axis=0,
        tiled=True,
    ).reshape(experts * capacity, features)
    half_size = lax.axis_size("pipe") // 2
    upper_half = (lax.axis_index("pipe") >= half_size).astype(jnp.int32)
    half_rows = dequant_half.shape[0]
    other_half = partner(dequant_half, "pipe")
    whole = jnp.where(
        upper_half == 1,
        jnp.concatenate([other_half, dequant_half], axis=0),
        jnp.concatenate([dequant_half, other_half], axis=0),
    )
    hidden = lax.dot_general(
        received, whole, (((1,), (1,)), ((), ())), preferred_element_type=jnp.float32
    ).astype(jnp.bfloat16)
    section_sum = lax.dot_general(
        activations, received, (((0,), (0,)), ((), ())), preferred_element_type=jnp.float32
    )
    their_part = lax.dynamic_slice_in_dim(
        section_sum, (1 - upper_half) * half_rows, half_rows, 0
    ).astype(jnp.bfloat16)
    received_part = partner(their_part, "pipe")
    own_part = lax.dynamic_slice_in_dim(section_sum, upper_half * half_rows, half_rows, 0)
    rounded = lax.optimization_barrier(own_part.astype(jnp.bfloat16)).astype(jnp.float32)
    weight_grad = (rounded + received_part.astype(jnp.float32)).astype(jnp.bfloat16)
    return hidden, weight_grad


def kernel(
    sections, experts, gates_hbm, routes_hbm, scales_hbm, x_hbm, act_hbm, weight_hbm,
    hidden_hbm, grad_hbm,
    gates_ref, routes_ref, scales_ref, hidden_ref, grad_ref, x_own, act, act_t, weight, whole, got, scaled, gate_out, gate_in, gate_wide,
    theirs, ours, arrived,
    load_sem, store_sem, row_send, row_recv, gate_send, gate_recv, w_send, w_recv, p_send, p_recv,
):
    section = lax.axis_index("pipe")
    me = lax.axis_index("expert")
    pair = lax.rem(section + sections // 2, sections)
    upper = section // (sections // 2)
    high, core = me // 2, lax.rem(me, 2)
    sibling = me + 1 - 2 * core
    last = experts // 2 - 1
    tokens, features = x_hbm.shape
    chunks = features // WIDTH
    slots, wide = act_hbm.shape
    half = wide // 2

    def rows_of(block):
        return pl.ds(pl.multiple_of(block * tokens, tokens), tokens)

    def columns(chunk):
        return pl.ds(pl.multiple_of(chunk * WIDTH, WIDTH), WIDTH)

    load_x = pltpu.make_async_copy(x_hbm, x_own, load_sem.at[0])
    load_w = pltpu.make_async_copy(weight_hbm, weight, load_sem.at[1])
    load_a = pltpu.make_async_copy(act_hbm, act, load_sem.at[2])
    load_g = pltpu.make_async_copy(gates_hbm, gates_ref, load_sem.at[3])
    load_r = pltpu.make_async_copy(routes_hbm, routes_ref, load_sem.at[4])
    load_s = pltpu.make_async_copy(scales_hbm, scales_ref, load_sem.at[5])
    for load in (load_g, load_r, load_x, load_s, load_w, load_a):
        load.start()

    barrier = pltpu.get_barrier_semaphore()
    for step in range(1, experts):
        peer = lax.rem(me + step, experts)
        pl.semaphore_signal(barrier, inc=1, device_id=(section, peer), device_id_type=MESH)
    pl.semaphore_signal(barrier, inc=1, device_id=(pair, me), device_id_type=MESH)

    load_g.wait()
    load_r.wait()
    for expert in range(experts):
        gate_out[expert] = jnp.sum(
            jnp.where(routes_ref[...] == expert, gates_ref[...], 0.0), axis=0, keepdims=True
        )
    gate_in[me] = gate_out[me]
    load_x.wait()
    pl.semaphore_wait(barrier, experts)

    def move(block, chunk, way, peer, from_own=False):
        source = x_own.at[:, columns(chunk)] if from_own else got.at[chunk, rows_of(block)]
        return pltpu.make_async_remote_copy(
            src_ref=source,
            dst_ref=got.at[chunk, rows_of(block)],
            send_sem=row_send.at[way, block, chunk],
            recv_sem=row_recv.at[block, chunk],
            device_id=(section, peer),
            device_id_type=MESH,
        )

    def send_own(chunk):
        @pl.when(high > 0)
        def _():
            move(me, chunk, 0, me - 2, True).start()

        @pl.when(high < last)
        def _():
            move(me, chunk, 1, me + 2, True).start()

        move(me, chunk, 2, sibling, True).start()

    def gate_copy(peer, source):
        return pltpu.make_async_remote_copy(
            src_ref=gate_out.at[peer],
            dst_ref=gate_in.at[source],
            send_sem=gate_send.at[peer],
            recv_sem=gate_recv.at[source],
            device_id=(section, peer),
            device_id_type=MESH,
        )

    def weight_copy(chunk, which):
        rows = pl.ds(pl.multiple_of(which * half, half), half)
        return pltpu.make_async_remote_copy(
            src_ref=whole.at[chunk, rows],
            dst_ref=whole.at[chunk, rows],
            send_sem=w_send.at[chunk],
            recv_sem=w_recv.at[chunk],
            device_id=(pair, me),
            device_id_type=MESH,
        )

    def part_copy(chunk):
        return pltpu.make_async_remote_copy(
            src_ref=theirs.at[chunk],
            dst_ref=arrived.at[chunk],
            send_sem=p_send.at[chunk],
            recv_sem=p_recv.at[chunk],
            device_id=(pair, me),
            device_id_type=MESH,
        )

    for step in range(1, experts):
        gate_copy(lax.rem(me + step, experts), me).start()
    send_own(0)
    send_own(1)

    load_w.wait()
    load_s.wait()
    for chunk in range(chunks):
        for row in range(half // QBLOCK):
            for part in range(WIDTH // QBLOCK):
                column = chunk * (WIDTH // QBLOCK) + part
                piece = weight[
                    row * QBLOCK : (row + 1) * QBLOCK, column * QBLOCK : (column + 1) * QBLOCK
                ]
                whole[
                    chunk,
                    pl.ds(pl.multiple_of(upper * half + row * QBLOCK, QBLOCK), QBLOCK),
                    part * QBLOCK : (part + 1) * QBLOCK,
                ] = (piece.astype(jnp.float32) * scales_ref[row, column]).astype(jnp.bfloat16)
        weight_copy(chunk, upper).start()

    load_a.wait()

    @pl.loop(0, slots // WIDTH)
    def _(tile):
        at = pl.ds(pl.multiple_of(tile * WIDTH, WIDTH), WIDTH)
        act_t[:, at] = act[at, :].T

    for step in range(1, experts):
        source = lax.rem(me + step, experts)
        gate_copy(source, source).wait_recv()

    for block in range(experts):
        gate_wide[block] = jnp.broadcast_to(gate_in[block], (QBLOCK, tokens)).T

    def apply_gate(block, chunk, rows):
        for part in range(WIDTH // QBLOCK):
            at = slice(part * QBLOCK, (part + 1) * QBLOCK)
            scaled[chunk, rows_of(block), at] = (
                gate_wide[block] * rows[:, at].astype(jnp.float32)
            ).astype(jnp.bfloat16)

    def landed(block, chunk):
        move(block, chunk, 2, sibling).wait_recv()

    def gate_landed(block, chunk):
        apply_gate(block, chunk, got[chunk, rows_of(block)])

    @pl.loop(0, chunks)
    def _(chunk):
        apply_gate(me, chunk, x_own[:, columns(chunk)])
        for step in range(1, experts // 2):
            @pl.when(high >= step)
            def _():
                block = me - 2 * step
                landed(block, chunk)

                @pl.when(high < last)
                def _():
                    move(block, chunk, 1, me + 2).start()

                move(block, chunk, 2, sibling).start()

            @pl.when(high + step <= last)
            def _():
                block = me + 2 * step
                landed(block, chunk)

                @pl.when(high > 0)
                def _():
                    move(block, chunk, 0, me - 2).start()

                move(block, chunk, 2, sibling).start()

            if step == 1:
                landed(sibling, chunk)
                gate_landed(sibling, chunk)

            @pl.when(high >= step)
            def _():
                block = me - 2 * step
                gate_landed(block, chunk)

            @pl.when(high + step <= last)
            def _():
                block = me + 2 * step
                gate_landed(block, chunk)

        @pl.when(chunk + 2 < chunks)
        def _():
            send_own(chunk + 2)

        for step in range(1, experts // 2):
            @pl.when(high >= step)
            def _():
                block = sibling - 2 * step
                landed(block, chunk)
                gate_landed(block, chunk)

            @pl.when(high + step <= last)
            def _():
                block = sibling + 2 * step
                landed(block, chunk)
                gate_landed(block, chunk)

        their_rows = pl.ds(pl.multiple_of((1 - upper) * half, half), half)
        theirs[chunk] = jnp.dot(
            act_t[their_rows, :], scaled[chunk], preferred_element_type=jnp.float32
        ).astype(jnp.bfloat16)
        part_copy(chunk).start()
        our_rows = pl.ds(pl.multiple_of(upper * half, half), half)
        ours[chunk] = jnp.dot(
            act_t[our_rows, :], scaled[chunk], preferred_element_type=jnp.float32
        ).astype(jnp.bfloat16)

    for chunk in range(chunks):
        weight_copy(chunk, 1 - upper).wait_recv()

    @pl.loop(0, slots // WIDTH)
    def _(tile):
        at = pl.ds(pl.multiple_of(tile * WIDTH, WIDTH), WIDTH)
        total = None
        for chunk in range(chunks):
            term = lax.dot_general(
                scaled[chunk, at],
                whole[chunk],
                (((1,), (1,)), ((), ())),
                preferred_element_type=jnp.float32,
            )
            total = term if total is None else total + term
        hidden_ref[at, :] = total.astype(jnp.bfloat16)

    store_h = pltpu.make_async_copy(hidden_ref, hidden_hbm, store_sem.at[0])
    store_h.start()

    for chunk in range(chunks):
        part_copy(chunk).wait_recv()
        grad_ref[:, chunk * WIDTH : (chunk + 1) * WIDTH] = (
            ours[chunk].astype(jnp.float32) + arrived[chunk].astype(jnp.float32)
        ).astype(jnp.bfloat16)
    store_g = pltpu.make_async_copy(grad_ref, grad_hbm, store_sem.at[1])
    store_g.start()

    for step in range(1, experts):
        gate_copy(lax.rem(me + step, experts), me).wait_send()

    @pl.loop(0, chunks)
    def _(chunk):
        part_copy(chunk).wait_send()
        weight_copy(chunk, upper).wait_send()

        @pl.when(high > 0)
        def _():
            move(me, chunk, 0, me - 2, True).wait_send()

        @pl.when(high < last)
        def _():
            move(me, chunk, 1, me + 2, True).wait_send()

        move(me, chunk, 2, sibling, True).wait_send()
        for step in range(1, experts // 2):
            @pl.when(high >= step)
            def _():
                block = me - 2 * step

                @pl.when(high < last)
                def _():
                    move(block, chunk, 1, me + 2).wait_send()

                move(block, chunk, 2, sibling).wait_send()

            @pl.when(high + step <= last)
            def _():
                block = me + 2 * step

                @pl.when(high > 0)
                def _():
                    move(block, chunk, 0, me - 2).wait_send()

                move(block, chunk, 2, sibling).wait_send()

    store_h.wait()
    store_g.wait()


def store(hidden_hbm, grad_hbm, hidden_out, grad_out, hidden_ref, grad_ref, in_sem, out_sem):
    ways = ((hidden_hbm, hidden_ref, hidden_out), (grad_hbm, grad_ref, grad_out))
    loads, stores = [], []
    for source, held, target in ways:
        rows = source.shape[0] // PIECES
        for piece in range(PIECES):
            at, place = pl.ds(piece * rows, rows), len(loads)
            loads.append(pltpu.make_async_copy(source.at[at], held.at[at], in_sem.at[place]))
            stores.append(pltpu.make_async_copy(held.at[at], target.at[at], out_sem.at[place]))
    for load in loads:
        load.start()
    for load, put in zip(loads, stores):
        load.wait()
        put.start()
    for put in stores:
        put.wait()


def every_expert(gradient, gate_rows, route_rows, activations, weight, scales):
    sections, experts = lax.axis_size("pipe"), lax.axis_size("expert")
    tokens, features = gradient.shape
    slots, wide = activations.shape
    half = weight.shape[0]
    chunks = features // WIDTH
    bf16, f32 = jnp.bfloat16, jnp.float32
    dma = pltpu.SemaphoreType.DMA
    shapes = (
        jax.ShapeDtypeStruct((slots, wide), bf16),
        jax.ShapeDtypeStruct((half, features), bf16),
    )
    results = pl.pallas_call(
        functools.partial(kernel, sections, experts),
        out_shape=shapes,
        in_specs=[pl.BlockSpec(memory_space=pltpu.HBM)] * 6,
        out_specs=(pl.BlockSpec(memory_space=pltpu.HBM),) * 2,
        scratch_shapes=[
            pltpu.VMEM(gate_rows.shape[::-1], f32),
            pltpu.VMEM(route_rows.shape[::-1], jnp.int32),
            pltpu.SMEM(scales.shape, f32),
            pltpu.VMEM((slots, wide), bf16),
            pltpu.VMEM((half, features), bf16),
            pltpu.VMEM((tokens, features), bf16),
            pltpu.VMEM((slots, wide), bf16),
            pltpu.VMEM((wide, slots), bf16),
            pltpu.VMEM((half, features), bf16),
            pltpu.VMEM((chunks, wide, WIDTH), bf16),
            pltpu.VMEM((chunks, slots, WIDTH), bf16),
            pltpu.VMEM((chunks, slots, WIDTH), bf16),
            pltpu.VMEM((experts, 1, tokens), f32),
            pltpu.VMEM((experts, 1, tokens), f32),
            pltpu.VMEM((experts, tokens, QBLOCK), f32),
            pltpu.VMEM((chunks, half, WIDTH), bf16),
            pltpu.VMEM((chunks, half, WIDTH), bf16),
            pltpu.VMEM((chunks, half, WIDTH), bf16),
            dma((6,)),
            dma((2,)),
            dma((3, experts, chunks)),
            dma((experts, chunks)),
            dma((experts,)),
            dma((experts,)),
            dma((chunks,)),
            dma((chunks,)),
            dma((chunks,)),
            dma((chunks,)),
        ],
        compiler_params=pltpu.CompilerParams(
            collective_id=0, has_side_effects=True, vmem_limit_bytes=ROOM
        ),
        cost_estimate=pl.CostEstimate(
            flops=4 * slots * wide * features,
            bytes_accessed=4 * slots * wide + 6 * half * features,
            transcendentals=0,
        ),
    )(gate_rows.T, route_rows.T, scales, gradient, activations, weight)
    return pl.pallas_call(
        store,
        out_shape=shapes,
        in_specs=[pl.BlockSpec(memory_space=pltpu.HBM)] * 2,
        out_specs=(pl.BlockSpec(memory_space=pltpu.HBM),) * 2,
        scratch_shapes=[
            pltpu.VMEM((slots, wide), bf16),
            pltpu.VMEM((half, features), bf16),
            dma((2 * PIECES,)),
            dma((2 * PIECES,)),
        ],
        compiler_params=pltpu.CompilerParams(vmem_limit_bytes=ROOM),
    )(*results)


def on_device(out_grad, gate_weights, routes, hidden_act, down_weight, block_scales):
    experts, sections = lax.axis_size("expert"), lax.axis_size("pipe")
    gradient, gate_rows, route_rows = out_grad[0, 0], gate_weights[0, 0], routes[0, 0]
    weight, scales = down_weight[0, 0], block_scales[0, 0]
    tokens, features = gradient.shape
    dense = (
        experts == route_rows.shape[1]
        and experts >= 4
        and experts % 2 == 0
        and sections % 2 == 0
        and tokens == QBLOCK
        and features % WIDTH == 0
        and features // WIDTH >= 2
        and weight.shape[0] % QBLOCK == 0
    )
    form = every_expert if dense else general
    hidden, weight_grad = form(
        gradient, gate_rows, route_rows, hidden_act[0, 0, 0], weight, scales
    )
    return hidden[None, None, None], weight_grad[None, None]


def solution(mesh):
    in_specs = (
        P("pipe", None, "expert", None),
        P("pipe", None, "expert", None),
        P("pipe", None, "expert", None),
        P("pipe", None, "expert", None, None),
        P("pipe", "expert", None, None),
        P("pipe", "expert", None, None),
    )
    out_specs = (P("pipe", None, "expert", None, None), P("pipe", "expert", None, None))
    return jax.shard_map(
        on_device, mesh=mesh, in_specs=in_specs, out_specs=out_specs, check_vma=False
    )
```

```python
import functools

import jax
import jax.numpy as jnp
from jax import lax
from jax.experimental import pallas as pl
from jax.experimental.pallas import tpu as pltpu
from jax.sharding import PartitionSpec as P

QBLOCK = 128
WIDTH = 512
TILE = 256
PIECES = 4
ROOM = 63 * 2**20
MESH = pl.DeviceIdType.MESH


def partner(block, axis):
    count = lax.axis_size(axis)
    route = [(place, (place + count // 2) % count) for place in range(count)]
    return lax.ppermute(block, axis, route)


def expand(scales):
    return jnp.repeat(jnp.repeat(scales, QBLOCK, axis=0), QBLOCK, axis=1)


def general(gradient, gate_rows, route_rows, activations, weight, scales):
    experts = lax.axis_size("expert")
    tok_count, features = gradient.shape
    top_count = route_rows.shape[1]
    capacity = tok_count * top_count // experts
    dequant_half = (weight.astype(jnp.float32) * expand(scales)).astype(jnp.bfloat16)
    named = route_rows[:, :, None] == jnp.arange(experts, dtype=jnp.int32)[None, None, :]
    gate_of = jnp.sum(jnp.where(named, gate_rows[:, :, None], 0.0), axis=1)
    member = jnp.any(named, axis=1)
    earlier = jnp.tril(jnp.ones((tok_count, tok_count), jnp.bfloat16), -1)
    rank = jnp.dot(earlier, member.astype(jnp.bfloat16), preferred_element_type=jnp.float32)
    rank = rank.astype(jnp.int32)
    places = jnp.arange(capacity, dtype=jnp.int32)[None, :, None]
    picked = member.T[:, None, :] & (rank.T[:, None, :] == places)
    slot_gate = jnp.sum(jnp.where(picked, gate_of.T[:, None, :], 0.0), axis=2)
    rows = jnp.dot(
        picked.reshape(experts * capacity, tok_count).astype(jnp.bfloat16),
        gradient,
        preferred_element_type=jnp.float32,
    )
    filled = (slot_gate.reshape(experts * capacity, 1) * rows).astype(jnp.bfloat16)
    received = lax.all_to_all(
        filled.reshape(experts, capacity, features),
        "expert",
        split_axis=0,
        concat_axis=0,
        tiled=True,
    ).reshape(experts * capacity, features)
    half_size = lax.axis_size("pipe") // 2
    upper_half = (lax.axis_index("pipe") >= half_size).astype(jnp.int32)
    half_rows = dequant_half.shape[0]
    other_half = partner(dequant_half, "pipe")
    whole = jnp.where(
        upper_half == 1,
        jnp.concatenate([other_half, dequant_half], axis=0),
        jnp.concatenate([dequant_half, other_half], axis=0),
    )
    hidden = lax.dot_general(
        received, whole, (((1,), (1,)), ((), ())), preferred_element_type=jnp.float32
    ).astype(jnp.bfloat16)
    section_sum = lax.dot_general(
        activations, received, (((0,), (0,)), ((), ())), preferred_element_type=jnp.float32
    )
    their_part = lax.dynamic_slice_in_dim(
        section_sum, (1 - upper_half) * half_rows, half_rows, 0
    ).astype(jnp.bfloat16)
    received_part = partner(their_part, "pipe")
    own_part = lax.dynamic_slice_in_dim(section_sum, upper_half * half_rows, half_rows, 0)
    rounded = lax.optimization_barrier(own_part.astype(jnp.bfloat16)).astype(jnp.float32)
    weight_grad = (rounded + received_part.astype(jnp.float32)).astype(jnp.bfloat16)
    return hidden, weight_grad


def kernel(
    sections, experts, gates_hbm, routes_hbm, scales_hbm, x_hbm, act_hbm, weight_hbm,
    hidden_hbm, grad_hbm,
    gates_ref, routes_ref, scales_ref, hidden_ref, grad_ref, x_own, act, act_t, weight, whole, got, scaled, gate_out, gate_in, gate_wide,
    theirs, ours, arrived,
    load_sem, store_sem, row_send, row_recv, gate_send, gate_recv, w_send, w_recv, p_send, p_recv,
):
    section = lax.axis_index("pipe")
    me = lax.axis_index("expert")
    pair = lax.rem(section + sections // 2, sections)
    upper = section // (sections // 2)
    high, core = me // 2, lax.rem(me, 2)
    sibling = me + 1 - 2 * core
    last = experts // 2 - 1
    tokens, features = x_hbm.shape
    chunks = features // WIDTH
    slots, wide = act_hbm.shape
    half = wide // 2

    def rows_of(block):
        return pl.ds(pl.multiple_of(block * tokens, tokens), tokens)

    def columns(chunk):
        return pl.ds(pl.multiple_of(chunk * WIDTH, WIDTH), WIDTH)

    load_x = pltpu.make_async_copy(x_hbm, x_own, load_sem.at[0])
    load_w = pltpu.make_async_copy(weight_hbm, weight, load_sem.at[1])
    load_a = pltpu.make_async_copy(act_hbm, act, load_sem.at[2])
    load_g = pltpu.make_async_copy(gates_hbm, gates_ref, load_sem.at[3])
    load_r = pltpu.make_async_copy(routes_hbm, routes_ref, load_sem.at[4])
    load_s = pltpu.make_async_copy(scales_hbm, scales_ref, load_sem.at[5])
    for load in (load_g, load_r, load_x, load_s, load_w, load_a):
        load.start()

    barrier = pltpu.get_barrier_semaphore()
    for step in range(1, experts):
        peer = lax.rem(me + step, experts)
        pl.semaphore_signal(barrier, inc=1, device_id=(section, peer), device_id_type=MESH)
    pl.semaphore_signal(barrier, inc=1, device_id=(pair, me), device_id_type=MESH)

    load_g.wait()
    load_r.wait()
    for expert in range(experts):
        gate_out[expert] = jnp.sum(
            jnp.where(routes_ref[...] == expert, gates_ref[...], 0.0), axis=0, keepdims=True
        )
    gate_in[me] = gate_out[me]
    load_x.wait()
    pl.semaphore_wait(barrier, experts)

    def move(block, chunk, way, peer, from_own=False):
        source = x_own.at[:, columns(chunk)] if from_own else got.at[chunk, rows_of(block)]
        return pltpu.make_async_remote_copy(
            src_ref=source,
            dst_ref=got.at[chunk, rows_of(block)],
            send_sem=row_send.at[way, block, chunk],
            recv_sem=row_recv.at[block, chunk],
            device_id=(section, peer),
            device_id_type=MESH,
        )

    def send_own(chunk):
        @pl.when(high > 0)
        def _():
            move(me, chunk, 0, me - 2, True).start()

        @pl.when(high < last)
        def _():
            move(me, chunk, 1, me + 2, True).start()

        move(me, chunk, 2, sibling, True).start()

    def gate_copy(peer, source):
        return pltpu.make_async_remote_copy(
            src_ref=gate_out.at[peer],
            dst_ref=gate_in.at[source],
            send_sem=gate_send.at[peer],
            recv_sem=gate_recv.at[source],
            device_id=(section, peer),
            device_id_type=MESH,
        )

    def weight_copy(chunk, which):
        rows = pl.ds(pl.multiple_of(which * half, half), half)
        return pltpu.make_async_remote_copy(
            src_ref=whole.at[chunk, rows],
            dst_ref=whole.at[chunk, rows],
            send_sem=w_send.at[chunk],
            recv_sem=w_recv.at[chunk],
            device_id=(pair, me),
            device_id_type=MESH,
        )

    def part_copy(chunk):
        return pltpu.make_async_remote_copy(
            src_ref=theirs.at[chunk],
            dst_ref=arrived.at[chunk],
            send_sem=p_send.at[chunk],
            recv_sem=p_recv.at[chunk],
            device_id=(pair, me),
            device_id_type=MESH,
        )

    for step in range(1, experts):
        gate_copy(lax.rem(me + step, experts), me).start()
    send_own(0)
    send_own(1)

    load_w.wait()
    load_s.wait()
    for chunk in range(chunks):
        for row in range(half // QBLOCK):
            for part in range(WIDTH // QBLOCK):
                column = chunk * (WIDTH // QBLOCK) + part
                piece = weight[
                    row * QBLOCK : (row + 1) * QBLOCK, column * QBLOCK : (column + 1) * QBLOCK
                ]
                whole[
                    chunk,
                    pl.ds(pl.multiple_of(upper * half + row * QBLOCK, QBLOCK), QBLOCK),
                    part * QBLOCK : (part + 1) * QBLOCK,
                ] = (piece.astype(jnp.float32) * scales_ref[row, column]).astype(jnp.bfloat16)
        weight_copy(chunk, upper).start()

    load_a.wait()

    @pl.loop(0, slots // TILE)
    def _(tile):
        at = pl.ds(pl.multiple_of(tile * TILE, TILE), TILE)
        act_t[:, at] = act[at, :].T

    for step in range(1, experts):
        source = lax.rem(me + step, experts)
        gate_copy(source, source).wait_recv()

    for block in range(experts):
        gate_wide[block] = jnp.broadcast_to(gate_in[block], (QBLOCK, tokens)).T

    def apply_gate(block, chunk, rows):
        for part in range(WIDTH // QBLOCK):
            at = slice(part * QBLOCK, (part + 1) * QBLOCK)
            scaled[chunk, rows_of(block), at] = (
                gate_wide[block] * rows[:, at].astype(jnp.float32)
            ).astype(jnp.bfloat16)

    def landed(block, chunk):
        move(block, chunk, 2, sibling).wait_recv()

    def gate_landed(block, chunk):
        apply_gate(block, chunk, got[chunk, rows_of(block)])

    @pl.loop(0, chunks)
    def _(chunk):
        apply_gate(me, chunk, x_own[:, columns(chunk)])
        for step in range(1, experts // 2):
            @pl.when(high >= step)
            def _():
                block = me - 2 * step
                landed(block, chunk)

                @pl.when(high < last)
                def _():
                    move(block, chunk, 1, me + 2).start()

                move(block, chunk, 2, sibling).start()

            @pl.when(high + step <= last)
            def _():
                block = me + 2 * step
                landed(block, chunk)

                @pl.when(high > 0)
                def _():
                    move(block, chunk, 0, me - 2).start()

                move(block, chunk, 2, sibling).start()

            if step == 1:
                landed(sibling, chunk)
                gate_landed(sibling, chunk)

            @pl.when(high >= step)
            def _():
                block = me - 2 * step
                gate_landed(block, chunk)

            @pl.when(high + step <= last)
            def _():
                block = me + 2 * step
                gate_landed(block, chunk)

        @pl.when(chunk + 2 < chunks)
        def _():
            send_own(chunk + 2)

        for step in range(1, experts // 2):
            @pl.when(high >= step)
            def _():
                block = sibling - 2 * step
                landed(block, chunk)
                gate_landed(block, chunk)

            @pl.when(high + step <= last)
            def _():
                block = sibling + 2 * step
                landed(block, chunk)
                gate_landed(block, chunk)

        their_rows = pl.ds(pl.multiple_of((1 - upper) * half, half), half)
        theirs[chunk] = jnp.dot(
            act_t[their_rows, :], scaled[chunk], preferred_element_type=jnp.float32
        ).astype(jnp.bfloat16)
        part_copy(chunk).start()
        our_rows = pl.ds(pl.multiple_of(upper * half, half), half)
        ours[chunk] = jnp.dot(
            act_t[our_rows, :], scaled[chunk], preferred_element_type=jnp.float32
        ).astype(jnp.bfloat16)

    for chunk in range(chunks):
        weight_copy(chunk, 1 - upper).wait_recv()

    @pl.loop(0, slots // TILE)
    def _(tile):
        at = pl.ds(pl.multiple_of(tile * TILE, TILE), TILE)
        total = None
        for chunk in range(chunks):
            term = lax.dot_general(
                scaled[chunk, at],
                whole[chunk],
                (((1,), (1,)), ((), ())),
                preferred_element_type=jnp.float32,
            )
            total = term if total is None else total + term
        hidden_ref[at, :] = total.astype(jnp.bfloat16)

    store_h = pltpu.make_async_copy(hidden_ref, hidden_hbm, store_sem.at[0])
    store_h.start()

    for chunk in range(chunks):
        part_copy(chunk).wait_recv()
        grad_ref[:, chunk * WIDTH : (chunk + 1) * WIDTH] = (
            ours[chunk].astype(jnp.float32) + arrived[chunk].astype(jnp.float32)
        ).astype(jnp.bfloat16)
    store_g = pltpu.make_async_copy(grad_ref, grad_hbm, store_sem.at[1])
    store_g.start()

    for step in range(1, experts):
        gate_copy(lax.rem(me + step, experts), me).wait_send()

    @pl.loop(0, chunks)
    def _(chunk):
        part_copy(chunk).wait_send()
        weight_copy(chunk, upper).wait_send()

        @pl.when(high > 0)
        def _():
            move(me, chunk, 0, me - 2, True).wait_send()

        @pl.when(high < last)
        def _():
            move(me, chunk, 1, me + 2, True).wait_send()

        move(me, chunk, 2, sibling, True).wait_send()
        for step in range(1, experts // 2):
            @pl.when(high >= step)
            def _():
                block = me - 2 * step

                @pl.when(high < last)
                def _():
                    move(block, chunk, 1, me + 2).wait_send()

                move(block, chunk, 2, sibling).wait_send()

            @pl.when(high + step <= last)
            def _():
                block = me + 2 * step

                @pl.when(high > 0)
                def _():
                    move(block, chunk, 0, me - 2).wait_send()

                move(block, chunk, 2, sibling).wait_send()

    store_h.wait()
    store_g.wait()


def store(hidden_hbm, grad_hbm, hidden_out, grad_out, hidden_ref, grad_ref, in_sem, out_sem):
    ways = ((hidden_hbm, hidden_ref, hidden_out), (grad_hbm, grad_ref, grad_out))
    loads, stores = [], []
    for source, held, target in ways:
        rows = source.shape[0] // PIECES
        for piece in range(PIECES):
            at, place = pl.ds(piece * rows, rows), len(loads)
            loads.append(pltpu.make_async_copy(source.at[at], held.at[at], in_sem.at[place]))
            stores.append(pltpu.make_async_copy(held.at[at], target.at[at], out_sem.at[place]))
    for load in loads:
        load.start()
    for load, put in zip(loads, stores):
        load.wait()
        put.start()
    for put in stores:
        put.wait()


def every_expert(gradient, gate_rows, route_rows, activations, weight, scales):
    sections, experts = lax.axis_size("pipe"), lax.axis_size("expert")
    tokens, features = gradient.shape
    slots, wide = activations.shape
    half = weight.shape[0]
    chunks = features // WIDTH
    bf16, f32 = jnp.bfloat16, jnp.float32
    dma = pltpu.SemaphoreType.DMA
    shapes = (
        jax.ShapeDtypeStruct((slots, wide), bf16),
        jax.ShapeDtypeStruct((half, features), bf16),
    )
    results = pl.pallas_call(
        functools.partial(kernel, sections, experts),
        out_shape=shapes,
        in_specs=[pl.BlockSpec(memory_space=pltpu.HBM)] * 6,
        out_specs=(pl.BlockSpec(memory_space=pltpu.HBM),) * 2,
        scratch_shapes=[
            pltpu.VMEM(gate_rows.shape[::-1], f32),
            pltpu.VMEM(route_rows.shape[::-1], jnp.int32),
            pltpu.SMEM(scales.shape, f32),
            pltpu.VMEM((slots, wide), bf16),
            pltpu.VMEM((half, features), bf16),
            pltpu.VMEM((tokens, features), bf16),
            pltpu.VMEM((slots, wide), bf16),
            pltpu.VMEM((wide, slots), bf16),
            pltpu.VMEM((half, features), bf16),
            pltpu.VMEM((chunks, wide, WIDTH), bf16),
            pltpu.VMEM((chunks, slots, WIDTH), bf16),
            pltpu.VMEM((chunks, slots, WIDTH), bf16),
            pltpu.VMEM((experts, 1, tokens), f32),
            pltpu.VMEM((experts, 1, tokens), f32),
            pltpu.VMEM((experts, tokens, QBLOCK), f32),
            pltpu.VMEM((chunks, half, WIDTH), bf16),
            pltpu.VMEM((chunks, half, WIDTH), bf16),
            pltpu.VMEM((chunks, half, WIDTH), bf16),
            dma((6,)),
            dma((2,)),
            dma((3, experts, chunks)),
            dma((experts, chunks)),
            dma((experts,)),
            dma((experts,)),
            dma((chunks,)),
            dma((chunks,)),
            dma((chunks,)),
            dma((chunks,)),
        ],
        compiler_params=pltpu.CompilerParams(
            collective_id=0, has_side_effects=True, vmem_limit_bytes=ROOM
        ),
        cost_estimate=pl.CostEstimate(
            flops=4 * slots * wide * features,
            bytes_accessed=4 * slots * wide + 6 * half * features,
            transcendentals=0,
        ),
    )(gate_rows.T, route_rows.T, scales, gradient, activations, weight)
    return pl.pallas_call(
        store,
        out_shape=shapes,
        in_specs=[pl.BlockSpec(memory_space=pltpu.HBM)] * 2,
        out_specs=(pl.BlockSpec(memory_space=pltpu.HBM),) * 2,
        scratch_shapes=[
            pltpu.VMEM((slots, wide), bf16),
            pltpu.VMEM((half, features), bf16),
            dma((2 * PIECES,)),
            dma((2 * PIECES,)),
        ],
        compiler_params=pltpu.CompilerParams(vmem_limit_bytes=ROOM),
    )(*results)


def on_device(out_grad, gate_weights, routes, hidden_act, down_weight, block_scales):
    experts, sections = lax.axis_size("expert"), lax.axis_size("pipe")
    gradient, gate_rows, route_rows = out_grad[0, 0], gate_weights[0, 0], routes[0, 0]
    weight, scales = down_weight[0, 0], block_scales[0, 0]
    tokens, features = gradient.shape
    dense = (
        experts == route_rows.shape[1]
        and experts >= 4
        and experts % 2 == 0
        and sections % 2 == 0
        and tokens == QBLOCK
        and features % WIDTH == 0
        and features // WIDTH >= 2
        and weight.shape[0] % QBLOCK == 0
    )
    form = every_expert if dense else general
    hidden, weight_grad = form(
        gradient, gate_rows, route_rows, hidden_act[0, 0, 0], weight, scales
    )
    return hidden[None, None, None], weight_grad[None, None]


def solution(mesh):
    in_specs = (
        P("pipe", None, "expert", None),
        P("pipe", None, "expert", None),
        P("pipe", None, "expert", None),
        P("pipe", None, "expert", None, None),
        P("pipe", "expert", None, None),
        P("pipe", "expert", None, None),
    )
    out_specs = (P("pipe", None, "expert", None, None), P("pipe", "expert", None, None))
    return jax.shard_map(
        on_device, mesh=mesh, in_specs=in_specs, out_specs=out_specs, check_vma=False
    )
```
